32 devices in a mesh: band: 2 (over y), sta: 4 (over z), grid: 4 (over x, core).
Axes of the slice: x: 2, y: 2, z: 4, core: 2. Of those that a mesh axis runs over, the one named last changes fastest.
Arguments:
- green_spectra: float32 [16, 256, 2, 1024], P('band', 'sta', None, 'grid'), parts along dimension 0, may hold values from -6 to 6
- source_power: float32 [16, 1024], P('band', 'grid'), parts along dimension 0, may hold values from 0.25 to 4
- partners: int32 [4, 2], P('sta'), may hold values from 0 to 3, as said below
- observed: float32 [4, 2, 16, 64, 128], P('sta', None, 'band'), parts along dimension 2, may hold values from -6 to 6
- region: int32 [16], P(('band', 'grid')), parts along dimension 0, may hold values 0 or 1
Outputs:
- gradient: float32 [16, 1024], P('band', 'grid'), parts along dimension 0
The draws below stay inside these ranges and needn't reach their ends.
There are 2 independent parts, one for each index of `band`. The reference program is written for one: setup_inputs(seed, part) draws one part's arguments, and reference() takes and returns one part's arrays. A program takes and returns all parts, laid end to end along the dimension named above; an argument that names none is the same for every part. Nothing has to cross between parts.
Inputs may be any that keep to these rules, and one draw needn't show every extreme that they name: `partners`: row a lists 2 distinct blocks, each within loop distance 1 of a among the 4 blocks (block b is at distance min((b - a) mod 4, (a - b) mod 4)); a itself is always listed, and so is one block at distance exactly 1.
All inputs are finite; a program needn't handle non-finite values. No bound on the sum of `region` on one device may be relied on, other than what follows from the above.
Results may differ from the reference program's by a relative error of at most 0.0003.
Values sent between devices are 32-bit elements; how exact they have to be, the bound alone decides.
A program may use at most 64 MiB of HBM per device.

```python
import math
import jax
import jax.numpy as jnp
from jax import lax

FREQ = 8
SB = 64
MBLK = 128
STATIONS = 256
NBLK = 4
NGRID = 1024
NMASK = 8
REACH = 1
NPAIR = 2


def draw_partners(key, part):
    key = jax.random.fold_in(key, 11)
    key_order, key_sign, key_shuffle = jax.random.split(key, 3)
    inner = jnp.concatenate([jnp.arange(1, REACH, dtype=jnp.int32), -jnp.arange(1, REACH, dtype=jnp.int32)])
    count = 2 * REACH - 2
    scores = jax.random.randint(key_order, (NBLK, count), 0, 1 << 20) * (count + 1) + jnp.arange(count, dtype=jnp.int32)[None, :]
    order = jnp.argsort(scores, axis=1)[:, :NPAIR - 2]
    picked = inner[order]
    signs = jax.random.randint(key_sign, (NBLK, 1), 0, 2) * 2 - 1
    offsets = jnp.concatenate([jnp.zeros((NBLK, 1), jnp.int32), signs * REACH, picked], axis=1)
    shuffle_scores = jax.random.randint(key_shuffle, (NBLK, NPAIR), 0, 1 << 20) * (NPAIR + 1) + jnp.arange(NPAIR, dtype=jnp.int32)[None, :]
    placing = jnp.argsort(shuffle_scores, axis=1)
    offsets = jnp.take_along_axis(offsets, placing, axis=1)
    rows = jnp.arange(NBLK, dtype=jnp.int32)[:, None]
    return ((rows + offsets) % NBLK).astype(jnp.int32)


def plant(entries, stream_key, low, top_value):
    longest = entries.shape.index(max(entries.shape))
    spots = []
    for shift in (0, 1):
        where = [jax.random.randint(jax.random.fold_in(stream_key, axis), (), 0, length) for axis, length in enumerate(entries.shape)]
        where[longest] = (where[longest] + shift) % entries.shape[longest]
        spots.append(tuple(where))
    return entries.at[spots[0]].set(low).at[spots[1]].set(top_value)


def steps_of(key, shape, cuts, smallest, high):
    factor_of, own = 1.0, jax.random.fold_in(key, 6)
    for position, blocks in cuts:
        steps = jnp.exp(jax.random.uniform(jax.random.fold_in(own, position), (blocks,), jnp.float32, smallest / len(cuts), high / len(cuts)))
        factor_of = factor_of * jnp.repeat(steps, shape[position] // blocks).reshape([-1 if axis == position else 1 for axis in range(len(shape))])
    return factor_of


def scatter_about(stream_key, dims, deviation, most, cuts=(), held_as=jnp.bfloat16):
    factor_of = steps_of(stream_key, dims, cuts, -0.22, 0.18) if cuts else 1.0
    values = jax.random.normal(stream_key, dims, jnp.float32) * deviation * factor_of
    return jnp.minimum(jnp.maximum(values, -most), most).astype(held_as)


def setup_inputs(seed: int = 0, part: int = 0) -> dict:
    streams_of = jax.random.split(jax.random.key(seed), 6)
    part_keys = jax.random.split(jax.random.fold_in(streams_of[5], part), 6)
    return {
        "green_spectra": scatter_about(part_keys[0], (FREQ, STATIONS, 2, NGRID), 1.0, 6.0, ((1, 4), (3, 4)), jnp.float32),
        "source_power": jnp.clip(jnp.exp(math.log(4.0) - 2.7725887 * jax.random.uniform(part_keys[1], (FREQ, NGRID), jnp.float32) ** steps_of(part_keys[1], (FREQ, NGRID), ((1, 4),), -0.2, 0.2)), 0.25, 4.0),
        "partners": draw_partners(jax.random.fold_in(streams_of[5], 71), part),
        "observed": scatter_about(part_keys[3], (NBLK, NPAIR, FREQ, SB, 2 * SB), 1.0, 6.0, ((0, 4),), jnp.float32),
        "region": plant((jax.random.randint(part_keys[4], (NMASK,), 0, 2) < 1).astype(jnp.int32), jax.random.fold_in(part_keys[4], 1), 0, 1),
    }


HIGH = lax.Precision.HIGHEST

def correlate(scaled, far, norm_scale):
    left_re = scaled[:, :, 0]
    left_im = scaled[:, :, 1]
    right_re = far[:, :, 0]
    right_im = far[:, :, 1]
    real_part = jnp.einsum('fit,fjt->fij', left_re, right_re, precision=HIGH) + jnp.einsum('fit,fjt->fij', left_im, right_im, precision=HIGH)
    imag_part = jnp.einsum('fit,fjt->fij', left_im, right_re, precision=HIGH) - jnp.einsum('fit,fjt->fij', left_re, right_im, precision=HIGH)
    return jnp.concatenate([real_part, imag_part], axis=-1) * norm_scale

def gradient_term(residual, near, far):
    width = residual.shape[1]
    res_re = residual[..., :width]
    res_im = residual[..., width:]
    near_re = near[:, :, 0]
    near_im = near[:, :, 1]
    mix_re = jnp.einsum('fij,fit->fjt', res_re, near_re, precision=HIGH) + jnp.einsum('fij,fit->fjt', res_im, near_im, precision=HIGH)
    mix_im = jnp.einsum('fij,fit->fjt', res_re, near_im, precision=HIGH) - jnp.einsum('fij,fit->fjt', res_im, near_re, precision=HIGH)
    return lax.optimization_barrier(jnp.sum(mix_re * far[:, :, 0] + mix_im * far[:, :, 1], axis=1))

def reference(green_spectra, source_power, partners, observed, region):
    norm_scale = 1.0 / math.sqrt(NGRID)
    eyes = jnp.concatenate([jnp.eye(SB, dtype=jnp.float32), jnp.eye(SB, dtype=jnp.float32)], axis=1)

    def visit(total, block_index):
        near = lax.dynamic_slice_in_dim(green_spectra, block_index * SB, SB, 1)
        scaled = near * source_power[:, None, None, :]
        for column in range(NPAIR):
            partner = partners[block_index, column]
            far = lax.dynamic_slice_in_dim(green_spectra, (partner * SB).astype(jnp.int32), SB, 1)
            self_flag = jnp.where(partner == block_index, 1.0, 0.0).astype(jnp.float32)
            keep = 1.0 - self_flag * eyes
            residual = (correlate(scaled, far, norm_scale) - observed[block_index, column]) * keep[None]
            total = total + gradient_term(residual, near, far)
        return (total, None)
    total, _ = lax.scan(visit, jnp.zeros((FREQ, NGRID), jnp.float32), jnp.arange(NBLK, dtype=jnp.int32))
    mask = jnp.repeat(region.astype(jnp.float32), MBLK)
    return total * (norm_scale / math.sqrt(NPAIR * SB)) * mask[None, :]
```

```python
import functools
import math

import jax
import jax.numpy as jnp
from jax import lax
from jax.experimental import pallas as pl
from jax.experimental.pallas import tpu as pltpu
from jax.sharding import PartitionSpec as P

MBLK = 128
MAX_REACH = 4
MESH = pl.DeviceIdType.MESH
F32 = jnp.float32
BF16 = jnp.bfloat16


def split(x):
    high = x.astype(BF16)
    return high, (x - high.astype(F32)).astype(BF16)


def dot3(left, right, contract):
    dot = functools.partial(
        lax.dot_general, dimension_numbers=(contract, ((), ())), preferred_element_type=F32
    )
    return dot(left[0], right[0]) + dot(left[0], right[1]) + dot(left[1], right[0])


def kernel(
    stations, tiles, reach, c_scale, out_scale,
    g_hbm, power_ref, partners_ref, obs_ref, region_ref, out_ref,
    near, far, wide, cpart, crecv, rfull, flip, pay, payrecv, tot, totrecv,
    load_sem, g_send, g_recv, pay_send, pay_recv, c_send, c_recv, r_send, r_recv, t_send, t_recv,
):
    freqs, rows, _ = g_hbm.shape
    block = obs_ref.shape[3]
    pairs = obs_ref.shape[1]
    cols = rows // (2 * block)
    tile = cols * 128
    own_rows = block // tiles
    me = lax.axis_index("sta")
    mine = lax.axis_index("grid")
    first = pl.multiple_of(mine * own_rows, own_rows)

    load = pltpu.make_async_copy(g_hbm, near, load_sem)
    load.start()

    barrier = pltpu.get_barrier_semaphore()
    for k in range(1, stations):
        pl.semaphore_signal(
            barrier, inc=1, device_id={"sta": lax.rem(me + k, stations)}, device_id_type=MESH
        )
    for k in range(1, tiles):
        pl.semaphore_signal(
            barrier, inc=1, device_id={"grid": lax.rem(mine + k, tiles)}, device_id_type=MESH
        )
    pl.semaphore_wait(barrier, stations - 1 + tiles - 1)

    def green_copy(d, f):
        return pltpu.make_async_remote_copy(
            src_ref=g_hbm.at[f], dst_ref=far.at[d - 1, f],
            send_sem=g_send.at[d - 1, f], recv_sem=g_recv.at[d - 1, f],
            device_id={"sta": lax.rem(me + d, stations)}, device_id_type=MESH,
        )

    def pay_copy(d):
        return pltpu.make_async_remote_copy(
            src_ref=pay.at[d - 1], dst_ref=payrecv.at[d - 1],
            send_sem=pay_send.at[d - 1], recv_sem=pay_recv.at[d - 1],
            device_id={"sta": lax.rem(me + d, stations)}, device_id_type=MESH,
        )

    def corr_copy(k, f):
        peer = lax.rem(mine + k, tiles)
        return pltpu.make_async_remote_copy(
            src_ref=cpart.at[f, peer], dst_ref=crecv.at[f, k],
            send_sem=c_send.at[k, f], recv_sem=c_recv.at[k, f],
            device_id={"grid": peer}, device_id_type=MESH,
        )

    def resid_copy(k, f, owner):
        return pltpu.make_async_remote_copy(
            src_ref=rfull.at[f, owner], dst_ref=rfull.at[f, owner],
            send_sem=r_send.at[k, f], recv_sem=r_recv.at[k, f],
            device_id={"grid": lax.rem(mine + k, tiles)}, device_id_type=MESH,
        )

    def total_copy(k):
        return pltpu.make_async_remote_copy(
            src_ref=tot, dst_ref=totrecv.at[k],
            send_sem=t_send.at[k], recv_sem=t_recv.at[k],
            device_id={"sta": lax.rem(me + k, stations)}, device_id_type=MESH,
        )

    def listed(q, target):
        return jnp.where(partners_ref[0, q] == target, 1.0, 0.0).astype(F32)

    early = min(2, freqs)
    for f in range(early):
        for d in range(1, reach + 1):
            green_copy(d, f).start()

    lane = lax.broadcasted_iota(jnp.int32, (own_rows, 2 * block), 1)
    sign = jnp.where(lane < block, 1.0, -1.0).astype(F32)
    for d in range(1, reach + 1):
        target = lax.rem(me + d, stations)
        flags = [listed(q, target) for q in range(pairs)]

        def flip_one(f, carry):
            chosen = flags[0] * obs_ref[0, 0, f]
            for q in range(1, pairs):
                chosen = chosen + flags[q] * obs_ref[0, q, f]
            square = jnp.concatenate([chosen, pltpu.roll(chosen, block, 1)], axis=0)
            flip[...] = square.T
            pay[d - 1, f] = flip[pl.ds(first, own_rows), :] * sign
            return carry

        lax.fori_loop(0, freqs, flip_one, 0)
        count = flags[0]
        for q in range(1, pairs):
            count = count + flags[q]
        pay[d - 1, freqs] = jnp.zeros((own_rows, 2 * block), F32) + count
        pay_copy(d).start()

    for f in range(early, freqs):
        for d in range(1, reach + 1):
            green_copy(d, f).start()

    load.wait()

    def parts(ref, f):
        out = []
        for part in range(2):
            pieces = [
                ref[f, pl.ds(2 * c + part, block, stride=2 * cols), :] for c in range(cols)
            ]
            out.append(jnp.concatenate(pieces, axis=1))
        return out

    def widen(real, imag, slot, f):
        rh, rl = split(real)
        ih, il = split(imag)
        for number, (re, im) in enumerate(((rh, ih), (rl, il))):
            wide[slot, f, number, 0:block] = jnp.concatenate([re, im], axis=1)
            wide[slot, f, number, block : 2 * block] = jnp.concatenate([-im, re], axis=1)

    def correlate(left, slot, f):
        right = (wide[slot, f, 0], wide[slot, f, 1])
        whole = dot3(left, right, ((1,), (1,))) * c_scale
        for k in range(tiles):
            cpart[f, k, slot] = whole[k * own_rows : (k + 1) * own_rows]

    def stage_corr(f):
        real, imag = parts(near, f)
        power = power_ref[pl.ds(f, 1), :]
        widen(real, imag, 0, f)
        left = split(jnp.concatenate([real * power, imag * power], axis=1))
        correlate(left, 0, f)
        for d in range(1, reach + 1):
            green_copy(d, f).wait_recv()
            real, imag = parts(far.at[d - 1], f)
            widen(real, imag, d, f)
            correlate(left, d, f)
        for k in range(1, tiles):
            corr_copy(k, f).start()

    row = lax.broadcasted_iota(jnp.int32, (own_rows, 2 * block), 0) + mine * own_rows
    keep = jnp.where(lax.rem(lane, block) == row, 0.0, 1.0).astype(F32)

    def observed_rows(f, target):
        chosen = listed(0, target) * obs_ref[0, 0, f, pl.ds(first, own_rows), :]
        for q in range(1, pairs):
            chosen = chosen + listed(q, target) * obs_ref[0, q, f, pl.ds(first, own_rows), :]
        return chosen

    def stage_resid(f):
        for k in range(1, tiles):
            corr_copy(k, f).wait_recv()
        for slot in range(reach + 1):
            total = cpart[f, mine, slot]
            for k in range(1, tiles):
                total = total + crecv[f, k, slot]
            target = lax.rem(me + stations - slot, stations)
            seen = observed_rows(f, target)
            if slot == 0:
                result = (total - seen) * keep
            else:
                weight = payrecv[slot - 1, freqs]
                for q in range(pairs):
                    weight = weight + listed(q, target)
                result = weight * total - (seen + payrecv[slot - 1, f])
            rfull[f, mine, slot] = result
        for k in range(1, tiles):
            resid_copy(k, f, mine).start()

    def stage_grad(f):
        for k in range(1, tiles):
            resid_copy(k, f, lax.rem(mine + tiles - k, tiles)).wait_recv()
        mixed = None
        for slot in range(reach + 1):
            resid = jnp.concatenate([rfull[f, k, slot] for k in range(tiles)], axis=0)
            term = dot3(split(resid), (wide[slot, f, 0], wide[slot, f, 1]), ((1,), (0,)))
            mixed = term if mixed is None else mixed + term
        real, imag = parts(near, f)
        line = jnp.sum(real * mixed[:, :tile] + imag * mixed[:, tile:], axis=0, keepdims=True)
        tot[pl.ds(f, 1), :] = line

    def step(s, carry):
        @pl.when(s < freqs)
        def _():
            stage_corr(s)

        @pl.when(s == 1)
        def _():
            for d in range(1, reach + 1):
                pay_copy(d).wait_recv()

        @pl.when(jnp.logical_and(s >= 1, s < freqs + 1))
        def _():
            stage_resid(s - 1)

        @pl.when(s >= 2)
        def _():
            stage_grad(s - 2)

        return carry

    lax.fori_loop(0, freqs + 2, step, 0)

    for k in range(1, stations):
        total_copy(k).start()

    def drain(f, carry):
        for d in range(1, reach + 1):
            green_copy(d, f).wait_send()
        for k in range(1, tiles):
            corr_copy(k, f).wait_send()
            resid_copy(k, f, mine).wait_send()
        return carry

    lax.fori_loop(0, freqs, drain, 0)
    for d in range(1, reach + 1):
        pay_copy(d).wait_send()
    summed = tot[...]
    for k in range(1, stations):
        total_copy(k).wait_recv()
        summed = summed + totrecv[k]
    for c in range(tile // MBLK):
        factor = region_ref[c].astype(F32) * out_scale
        span = slice(c * MBLK, (c + 1) * MBLK)
        out_ref[:, span] = summed[:, span] * factor
    for k in range(1, stations):
        total_copy(k).wait_send()


def shards(green_spectra, source_power, partners, observed, region):
    stations = lax.axis_size("sta")
    tiles = lax.axis_size("grid")
    reach = min(MAX_REACH, (stations - 1) // 2)
    freqs, block, _, tile = green_spectra.shape
    pairs = partners.shape[1]
    cols = tile // 128
    own_rows = block // tiles
    slots = reach + 1
    c_scale = 1.0 / math.sqrt(tile * tiles)
    out_scale = c_scale / math.sqrt(pairs * block)
    green = green_spectra.reshape(freqs, block, 2, cols, 128)
    green = green.transpose(0, 1, 3, 2, 4).reshape(freqs, block * cols * 2, 128)
    vmem = pl.BlockSpec(memory_space=pltpu.VMEM)
    smem = pl.BlockSpec(memory_space=pltpu.SMEM)
    dma = pltpu.SemaphoreType.DMA
    return pl.pallas_call(
        functools.partial(kernel, stations, tiles, reach, c_scale, out_scale),
        out_shape=jax.ShapeDtypeStruct((freqs, tile), F32),
        in_specs=[pl.BlockSpec(memory_space=pl.ANY), vmem, smem, vmem, smem],
        out_specs=vmem,
        scratch_shapes=[
            pltpu.VMEM(green.shape, F32),
            pltpu.VMEM((reach,) + green.shape, F32),
            pltpu.VMEM((slots, freqs, 2, 2 * block, 2 * tile), BF16),
            pltpu.VMEM((freqs, tiles, slots, own_rows, 2 * block), F32),
            pltpu.VMEM((freqs, tiles, slots, own_rows, 2 * block), F32),
            pltpu.VMEM((freqs, tiles, slots, own_rows, 2 * block), F32),
            pltpu.VMEM((2 * block, 2 * block), F32),
            pltpu.VMEM((reach, freqs + 1, own_rows, 2 * block), F32),
            pltpu.VMEM((reach, freqs + 1, own_rows, 2 * block), F32),
            pltpu.VMEM((freqs, tile), F32),
            pltpu.VMEM((stations, freqs, tile), F32),
            dma,
            dma((reach, freqs)), dma((reach, freqs)),
            dma((reach,)), dma((reach,)),
            dma((tiles, freqs)), dma((tiles, freqs)),
            dma((tiles, freqs)), dma((tiles, freqs)),
            dma((stations,)), dma((stations,)),
        ],
        compiler_params=pltpu.CompilerParams(
            collective_id=0, has_side_effects=True, vmem_limit_bytes=48 * 1024 * 1024
        ),
    )(green, source_power, partners, observed, region)


def solution(mesh):
    in_specs = (
        P("band", "sta", None, "grid"),
        P("band", "grid"),
        P("sta", None),
        P("sta", None, "band", None, None),
        P(("band", "grid")),
    )
    out_specs = P("band", "grid")
    return jax.shard_map(shards, mesh=mesh, in_specs=in_specs, out_specs=out_specs, check_vma=False)
```

```python
import functools
import math

import jax
import jax.numpy as jnp
from jax import lax
from jax.experimental import pallas as pl
from jax.experimental.pallas import tpu as pltpu
from jax.sharding import PartitionSpec as P

MBLK = 128
MAX_REACH = 4
MESH = pl.DeviceIdType.MESH
F32 = jnp.float32
BF16 = jnp.bfloat16


def split(x):
    high = x.astype(BF16)
    return high, (x - high.astype(F32)).astype(BF16)


def dot3(left, right, contract):
    dot = functools.partial(
        lax.dot_general, dimension_numbers=(contract, ((), ())), preferred_element_type=F32
    )
    return dot(left[0], right[0]) + dot(left[0], right[1]) + dot(left[1], right[0])


def kernel(
    stations, tiles, reach, c_scale, out_scale,
    g_hbm, power_hbm, partners_hbm, obs_hbm, region_hbm, out_ref,
    power_ref, partners_ref, obs_ref, region_ref, near, lefts, far, wide, cpart, crecv, rfull, flip, pay, payrecv, tot, totrecv,
    load_sem, small_sem, g_send, g_recv, pay_send, pay_recv, c_send, c_recv, r_send, r_recv, t_send, t_recv,
):
    freqs, rows, _ = g_hbm.shape
    block = obs_ref.shape[3]
    pairs = obs_ref.shape[1]
    cols = rows // (2 * block)
    tile = cols * 128
    own_rows = block // tiles
    me = lax.axis_index("sta")
    mine = lax.axis_index("grid")
    first = pl.multiple_of(mine * own_rows, own_rows)

    load = pltpu.make_async_copy(g_hbm, near, load_sem)
    load.start()
    small = [
        pltpu.make_async_copy(source, target, small_sem.at[number])
        for number, (source, target) in enumerate((
            (partners_hbm, partners_ref), (obs_hbm, obs_ref),
            (power_hbm, power_ref), (region_hbm, region_ref),
        ))
    ]
    for copy in small:
        copy.start()

    barrier = pltpu.get_barrier_semaphore()
    for k in range(1, stations):
        pl.semaphore_signal(
            barrier, inc=1, device_id={"sta": lax.rem(me + k, stations)}, device_id_type=MESH
        )
    for k in range(1, tiles):
        pl.semaphore_signal(
            barrier, inc=1, device_id={"grid": lax.rem(mine + k, tiles)}, device_id_type=MESH
        )
    pl.semaphore_wait(barrier, stations - 1 + tiles - 1)

    def green_copy(d, f):
        return pltpu.make_async_remote_copy(
            src_ref=g_hbm.at[f], dst_ref=far.at[d - 1, f],
            send_sem=g_send.at[d - 1, f], recv_sem=g_recv.at[d - 1, f],
            device_id={"sta": lax.rem(me + d, stations)}, device_id_type=MESH,
        )

    def pay_copy(d):
        return pltpu.make_async_remote_copy(
            src_ref=pay.at[d - 1], dst_ref=payrecv.at[d - 1],
            send_sem=pay_send.at[d - 1], recv_sem=pay_recv.at[d - 1],
            device_id={"sta": lax.rem(me + d, stations)}, device_id_type=MESH,
        )

    def corr_copy(k, f):
        peer = lax.rem(mine + k, tiles)
        return pltpu.make_async_remote_copy(
            src_ref=cpart.at[f, peer], dst_ref=crecv.at[f, k],
            send_sem=c_send.at[k, f], recv_sem=c_recv.at[k, f],
            device_id={"grid": peer}, device_id_type=MESH,
        )

    def resid_copy(k, f, owner):
        return pltpu.make_async_remote_copy(
            src_ref=rfull.at[f, owner], dst_ref=rfull.at[f, owner],
            send_sem=r_send.at[k, f], recv_sem=r_recv.at[k, f],
            device_id={"grid": lax.rem(mine + k, tiles)}, device_id_type=MESH,
        )

    def total_copy(k):
        return pltpu.make_async_remote_copy(
            src_ref=tot, dst_ref=totrecv.at[k],
            send_sem=t_send.at[k], recv_sem=t_recv.at[k],
            device_id={"sta": lax.rem(me + k, stations)}, device_id_type=MESH,
        )

    def listed(q, target):
        return jnp.where(partners_ref[0, q] == target, 1.0, 0.0).astype(F32)

    early = min(2, freqs)
    for f in range(early):
        for d in range(1, reach + 1):
            green_copy(d, f).start()

    for copy in small:
        copy.wait()

    lane = lax.broadcasted_iota(jnp.int32, (own_rows, 2 * block), 1)
    sign = jnp.where(lane < block, 1.0, -1.0).astype(F32)
    for d in range(1, reach + 1):
        target = lax.rem(me + d, stations)
        flags = [listed(q, target) for q in range(pairs)]

        def flip_one(f, carry):
            chosen = flags[0] * obs_ref[0, 0, f]
            for q in range(1, pairs):
                chosen = chosen + flags[q] * obs_ref[0, q, f]
            square = jnp.concatenate([chosen, pltpu.roll(chosen, block, 1)], axis=0)
            flip[...] = square.T
            pay[d - 1, f] = flip[pl.ds(first, own_rows), :] * sign
            return carry

        lax.fori_loop(0, freqs, flip_one, 0)
        count = flags[0]
        for q in range(1, pairs):
            count = count + flags[q]
        pay[d - 1, freqs] = jnp.zeros((own_rows, 2 * block), F32) + count
        pay_copy(d).start()

    for f in range(early, freqs):
        for d in range(1, reach + 1):
            green_copy(d, f).start()

    load.wait()

    def parts(ref, f):
        out = []
        for part in range(2):
            pieces = [
                ref[f, pl.ds(2 * c + part, block, stride=2 * cols), :] for c in range(cols)
            ]
            out.append(jnp.concatenate(pieces, axis=1))
        return out

    def widen(real, imag, slot, f):
        rh, rl = split(real)
        ih, il = split(imag)
        for number, (re, im) in enumerate(((rh, ih), (rl, il))):
            wide[slot, f, number, 0:block] = jnp.concatenate([re, im], axis=1)
            wide[slot, f, number, block : 2 * block] = jnp.concatenate([-im, re], axis=1)

    def correlate(left, slot, f):
        right = (wide[slot, f, 0], wide[slot, f, 1])
        whole = dot3(left, right, ((1,), (1,))) * c_scale
        for k in range(tiles):
            cpart[f, k, slot] = whole[k * own_rows : (k + 1) * own_rows]

    def stage_self(f):
        real, imag = parts(near, f)
        power = power_ref[pl.ds(f, 1), :]
        widen(real, imag, 0, f)
        high, low = split(jnp.concatenate([real * power, imag * power], axis=1))
        lefts[f, 0] = high
        lefts[f, 1] = low
        correlate((high, low), 0, f)

    def stage_cross(f):
        left = (lefts[f, 0], lefts[f, 1])
        for d in range(1, reach + 1):
            green_copy(d, f).wait_recv()
            real, imag = parts(far.at[d - 1], f)
            widen(real, imag, d, f)
            correlate(left, d, f)
        for k in range(1, tiles):
            corr_copy(k, f).start()

    row = lax.broadcasted_iota(jnp.int32, (own_rows, 2 * block), 0) + mine * own_rows
    keep = jnp.where(lax.rem(lane, block) == row, 0.0, 1.0).astype(F32)

    def observed_rows(f, target):
        chosen = listed(0, target) * obs_ref[0, 0, f, pl.ds(first, own_rows), :]
        for q in range(1, pairs):
            chosen = chosen + listed(q, target) * obs_ref[0, q, f, pl.ds(first, own_rows), :]
        return chosen

    def stage_resid(f):
        for k in range(1, tiles):
            corr_copy(k, f).wait_recv()
        for slot in range(reach + 1):
            total = cpart[f, mine, slot]
            for k in range(1, tiles):
                total = total + crecv[f, k, slot]
            target = lax.rem(me + stations - slot, stations)
            seen = observed_rows(f, target)
            if slot == 0:
                result = (total - seen) * keep
            else:
                weight = payrecv[slot - 1, freqs]
                for q in range(pairs):
                    weight = weight + listed(q, target)
                result = weight * total - (seen + payrecv[slot - 1, f])
            rfull[f, mine, slot] = result
        for k in range(1, tiles):
            resid_copy(k, f, mine).start()

    def stage_grad(f):
        for k in range(1, tiles):
            resid_copy(k, f, lax.rem(mine + tiles - k, tiles)).wait_recv()
        mixed = None
        for slot in range(reach + 1):
            resid = jnp.concatenate([rfull[f, k, slot] for k in range(tiles)], axis=0)
            term = dot3(split(resid), (wide[slot, f, 0], wide[slot, f, 1]), ((1,), (0,)))
            mixed = term if mixed is None else mixed + term
        real, imag = parts(near, f)
        line = jnp.sum(real * mixed[:, :tile] + imag * mixed[:, tile:], axis=0, keepdims=True)
        tot[pl.ds(f, 1), :] = line

    resid_lag, grad_lag = 1, 2

    def step(s, carry):
        @pl.when(s < freqs)
        def _():
            stage_self(s)
            stage_cross(s)

        @pl.when(s == resid_lag)
        def _():
            for d in range(1, reach + 1):
                pay_copy(d).wait_recv()

        @pl.when(jnp.logical_and(s >= resid_lag, s < freqs + resid_lag))
        def _():
            stage_resid(s - resid_lag)

        @pl.when(s >= grad_lag)
        def _():
            stage_grad(s - grad_lag)

        return carry

    lax.fori_loop(0, freqs + grad_lag, step, 0)

    for k in range(1, stations):
        total_copy(k).start()

    def drain(f, carry):
        for d in range(1, reach + 1):
            green_copy(d, f).wait_send()
        for k in range(1, tiles):
            corr_copy(k, f).wait_send()
            resid_copy(k, f, mine).wait_send()
        return carry

    lax.fori_loop(0, freqs, drain, 0)
    for d in range(1, reach + 1):
        pay_copy(d).wait_send()
    summed = tot[...]
    for k in range(1, stations):
        total_copy(k).wait_recv()
        summed = summed + totrecv[k]
    for c in range(tile // MBLK):
        factor = region_ref[c].astype(F32) * out_scale
        span = slice(c * MBLK, (c + 1) * MBLK)
        out_ref[:, span] = summed[:, span] * factor
    for k in range(1, stations):
        total_copy(k).wait_send()


def shards(green_spectra, source_power, partners, observed, region):
    stations = lax.axis_size("sta")
    tiles = lax.axis_size("grid")
    reach = min(MAX_REACH, (stations - 1) // 2)
    freqs, block, _, tile = green_spectra.shape
    pairs = partners.shape[1]
    cols = tile // 128
    own_rows = block // tiles
    slots = reach + 1
    c_scale = 1.0 / math.sqrt(tile * tiles)
    out_scale = c_scale / math.sqrt(pairs * block)
    green = green_spectra.reshape(freqs, block, 2, cols, 128)
    green = green.transpose(0, 1, 3, 2, 4).reshape(freqs, block * cols * 2, 128)
    vmem = pl.BlockSpec(memory_space=pltpu.VMEM)
    dma = pltpu.SemaphoreType.DMA
    return pl.pallas_call(
        functools.partial(kernel, stations, tiles, reach, c_scale, out_scale),
        out_shape=jax.ShapeDtypeStruct((freqs, tile), F32),
        in_specs=[pl.BlockSpec(memory_space=pl.ANY)] * 5,
        out_specs=vmem,
        scratch_shapes=[
            pltpu.VMEM(source_power.shape, F32),
            pltpu.SMEM(partners.shape, jnp.int32),
            pltpu.VMEM(observed.shape, F32),
            pltpu.SMEM(region.shape, jnp.int32),
            pltpu.VMEM(green.shape, F32),
            pltpu.VMEM((freqs, 2, block, 2 * tile), BF16),
            pltpu.VMEM((reach,) + green.shape, F32),
            pltpu.VMEM((slots, freqs, 2, 2 * block, 2 * tile), BF16),
            pltpu.VMEM((freqs, tiles, slots, own_rows, 2 * block), F32),
            pltpu.VMEM((freqs, tiles, slots, own_rows, 2 * block), F32),
            pltpu.VMEM((freqs, tiles, slots, own_rows, 2 * block), F32),
            pltpu.VMEM((2 * block, 2 * block), F32),
            pltpu.VMEM((reach, freqs + 1, own_rows, 2 * block), F32),
            pltpu.VMEM((reach, freqs + 1, own_rows, 2 * block), F32),
            pltpu.VMEM((freqs, tile), F32),
            pltpu.VMEM((stations, freqs, tile), F32),
            dma,
            dma((4,)),
            dma((reach, freqs)), dma((reach, freqs)),
            dma((reach,)), dma((reach,)),
            dma((tiles, freqs)), dma((tiles, freqs)),
            dma((tiles, freqs)), dma((tiles, freqs)),
            dma((stations,)), dma((stations,)),
        ],
        compiler_params=pltpu.CompilerParams(
            collective_id=0, has_side_effects=True, vmem_limit_bytes=60 * 1024 * 1024
        ),
    )(green, source_power, partners, observed, region)


def solution(mesh):
    in_specs = (
        P("band", "sta", None, "grid"),
        P("band", "grid"),
        P("sta", None),
        P("sta", None, "band", None, None),
        P(("band", "grid")),
    )
    out_specs = P("band", "grid")
    return jax.shard_map(shards, mesh=mesh, in_specs=in_specs, out_specs=out_specs, check_vma=False)
```

```python
import functools
import math

import jax
import jax.numpy as jnp
from jax import lax
from jax.experimental import pallas as pl
from jax.experimental.pallas import tpu as pltpu
from jax.sharding import PartitionSpec as P

MBLK = 128
MAX_REACH = 4
MESH = pl.DeviceIdType.MESH
F32 = jnp.float32
BF16 = jnp.bfloat16


def split(x):
    high = x.astype(BF16)
    return high, (x - high.astype(F32)).astype(BF16)


def dot3(left, right, contract):
    dot = functools.partial(
        lax.dot_general, dimension_numbers=(contract, ((), ())), preferred_element_type=F32
    )
    return dot(left[0], right[0]) + dot(left[0], right[1]) + dot(left[1], right[0])


def kernel(
    stations, tiles, reach, c_scale,
    g_hbm, power_hbm, partners_hbm, obs_hbm, out_ref,
    power_ref, partners_ref, obs_ref, near, lefts, far, wide, cself, cselfrecv, rself, cpart, crecv, rfull, flip, pay, payrecv, tot,
    load_sem, small_sem, own_sem, g_send, g_recv, pay_send, pay_recv, cs_send, cs_recv, rs_send, rs_recv,
    c_send, c_recv, r_send, r_recv, t_send, t_recv,
):
    freqs, rows, _ = g_hbm.shape
    block = obs_ref.shape[3]
    pairs = obs_ref.shape[1]
    cols = rows // (2 * block)
    tile = cols * 128
    own_rows = block // tiles
    me = lax.axis_index("sta")
    mine = lax.axis_index("grid")
    first = pl.multiple_of(mine * own_rows, own_rows)

    barrier = pltpu.get_barrier_semaphore()
    for k in range(1, stations):
        pl.semaphore_signal(
            barrier, inc=1, device_id={"sta": lax.rem(me + k, stations)}, device_id_type=MESH
        )
    for k in range(1, tiles):
        pl.semaphore_signal(
            barrier, inc=1, device_id={"grid": lax.rem(mine + k, tiles)}, device_id_type=MESH
        )

    load = pltpu.make_async_copy(g_hbm, near, load_sem)
    load.start()
    small = [
        pltpu.make_async_copy(source, target, small_sem.at[number])
        for number, (source, target) in enumerate((
            (partners_hbm, partners_ref), (obs_hbm, obs_ref),
            (power_hbm, power_ref),
        ))
    ]
    for copy in small:
        copy.start()

    pl.semaphore_wait(barrier, stations - 1 + tiles - 1)

    def green_copy(d, f):
        return pltpu.make_async_remote_copy(
            src_ref=g_hbm.at[f], dst_ref=far.at[d - 1, f],
            send_sem=g_send.at[d - 1, f], recv_sem=g_recv.at[d - 1, f],
            device_id={"sta": lax.rem(me + d, stations)}, device_id_type=MESH,
        )

    def pay_copy(d):
        return pltpu.make_async_remote_copy(
            src_ref=pay.at[d - 1], dst_ref=payrecv.at[d - 1],
            send_sem=pay_send.at[d - 1], recv_sem=pay_recv.at[d - 1],
            device_id={"sta": lax.rem(me + d, stations)}, device_id_type=MESH,
        )

    def corr_copy(k, f):
        peer = lax.rem(mine + k, tiles)
        return pltpu.make_async_remote_copy(
            src_ref=cpart.at[f, peer], dst_ref=crecv.at[f, k],
            send_sem=c_send.at[k, f], recv_sem=c_recv.at[k, f],
            device_id={"grid": peer}, device_id_type=MESH,
        )

    def resid_copy(k, f, owner):
        return pltpu.make_async_remote_copy(
            src_ref=rfull.at[f, owner], dst_ref=rfull.at[f, owner],
            send_sem=r_send.at[k, f], recv_sem=r_recv.at[k, f],
            device_id={"grid": lax.rem(mine + k, tiles)}, device_id_type=MESH,
        )

    def self_corr_copy(k):
        peer = lax.rem(mine + k, tiles)
        return pltpu.make_async_remote_copy(
            src_ref=cself.at[peer], dst_ref=cselfrecv.at[k],
            send_sem=cs_send.at[k], recv_sem=cs_recv.at[k],
            device_id={"grid": peer}, device_id_type=MESH,
        )

    def self_resid_copy(k, owner):
        return pltpu.make_async_remote_copy(
            src_ref=rself.at[owner], dst_ref=rself.at[owner],
            send_sem=rs_send.at[k], recv_sem=rs_recv.at[k],
            device_id={"grid": lax.rem(mine + k, tiles)}, device_id_type=MESH,
        )

    def total_copy(k):
        return pltpu.make_async_remote_copy(
            src_ref=tot, dst_ref=out_ref.at[k],
            send_sem=t_send.at[k], recv_sem=t_recv.at[k],
            device_id={"sta": lax.rem(me + k, stations)}, device_id_type=MESH,
        )

    def listed(q, target):
        return jnp.where(partners_ref[0, q] == target, 1.0, 0.0).astype(F32)

    early = min(2, freqs)
    for f in range(early):
        for d in range(1, reach + 1):
            green_copy(d, f).start()

    for copy in small:
        copy.wait()

    lane = lax.broadcasted_iota(jnp.int32, (own_rows, 2 * block), 1)
    sign = jnp.where(lane < block, 1.0, -1.0).astype(F32)
    for d in range(1, reach + 1):
        target = lax.rem(me + d, stations)
        flags = [listed(q, target) for q in range(pairs)]

        def flip_one(f, carry):
            chosen = flags[0] * obs_ref[0, 0, f]
            for q in range(1, pairs):
                chosen = chosen + flags[q] * obs_ref[0, q, f]
            square = jnp.concatenate([chosen, pltpu.roll(chosen, block, 1)], axis=0)
            flip[...] = square.T
            pay[d - 1, f] = flip[pl.ds(first, own_rows), :] * sign
            return carry

        lax.fori_loop(0, freqs, flip_one, 0)
        count = flags[0]
        for q in range(1, pairs):
            count = count + flags[q]
        pay[d - 1, freqs] = jnp.zeros((own_rows, 2 * block), F32) + count
        pay_copy(d).start()

    for f in range(early, freqs):
        for d in range(1, reach + 1):
            green_copy(d, f).start()

    load.wait()

    def parts(ref, f):
        out = []
        for part in range(2):
            pieces = [
                ref[f, pl.ds(2 * c + part, block, stride=2 * cols), :] for c in range(cols)
            ]
            out.append(jnp.concatenate(pieces, axis=1))
        return out

    def widen(real, imag, slot, f):
        rh, rl = split(real)
        ih, il = split(imag)
        for number, (re, im) in enumerate(((rh, ih), (rl, il))):
            wide[slot, f, number, 0:block] = jnp.concatenate([re, im], axis=1)
            wide[slot, f, number, block : 2 * block] = jnp.concatenate([-im, re], axis=1)

    def correlate(left, slot, f):
        right = (wide[slot, f, 0], wide[slot, f, 1])
        whole = dot3(left, right, ((1,), (1,))) * c_scale
        for k in range(tiles):
            piece = whole[k * own_rows : (k + 1) * own_rows]
            if slot == 0:
                cself[k, f] = piece
            else:
                cpart[f, k, slot - 1] = piece

    def stage_self(f):
        real, imag = parts(near, f)
        power = power_ref[pl.ds(f, 1), :]
        widen(real, imag, 0, f)
        high, low = split(jnp.concatenate([real * power, imag * power], axis=1))
        lefts[f, 0] = high
        lefts[f, 1] = low
        correlate((high, low), 0, f)

    def stage_cross(f):
        left = (lefts[f, 0], lefts[f, 1])
        for d in range(1, reach + 1):
            green_copy(d, f).wait_recv()
            real, imag = parts(far.at[d - 1], f)
            widen(real, imag, d, f)
            correlate(left, d, f)
        for k in range(1, tiles):
            corr_copy(k, f).start()

    row = lax.broadcasted_iota(jnp.int32, (own_rows, 2 * block), 0) + mine * own_rows
    keep = jnp.where(lax.rem(lane, block) == row, 0.0, 1.0).astype(F32)

    def observed_rows(f, target):
        chosen = listed(0, target) * obs_ref[0, 0, f, pl.ds(first, own_rows), :]
        for q in range(1, pairs):
            chosen = chosen + listed(q, target) * obs_ref[0, q, f, pl.ds(first, own_rows), :]
        return chosen

    def self_resid():
        for k in range(1, tiles):
            self_corr_copy(k).wait_recv()

        def one(f, carry):
            total = cself[mine, f]
            for k in range(1, tiles):
                total = total + cselfrecv[k, f]
            rself[mine, f] = (total - observed_rows(f, me)) * keep
            return carry

        lax.fori_loop(0, freqs, one, 0)
        for k in range(1, tiles):
            self_resid_copy(k, mine).start()

    def stage_resid(f):
        for k in range(1, tiles):
            corr_copy(k, f).wait_recv()
        for d in range(1, reach + 1):
            total = cpart[f, mine, d - 1]
            for k in range(1, tiles):
                total = total + crecv[f, k, d - 1]
            target = lax.rem(me + stations - d, stations)
            weight = payrecv[d - 1, freqs]
            for q in range(pairs):
                weight = weight + listed(q, target)
            seen = observed_rows(f, target) + payrecv[d - 1, f]
            rfull[f, mine, d - 1] = weight * total - seen
        for k in range(1, tiles):
            resid_copy(k, f, mine).start()

    def stage_grad(f):
        for k in range(1, tiles):
            resid_copy(k, f, lax.rem(mine + tiles - k, tiles)).wait_recv()
        mixed = None
        for slot in range(reach + 1):
            pieces = [rself[k, f] if slot == 0 else rfull[f, k, slot - 1] for k in range(tiles)]
            resid = jnp.concatenate(pieces, axis=0)
            term = dot3(split(resid), (wide[slot, f, 0], wide[slot, f, 1]), ((1,), (0,)))
            mixed = term if mixed is None else mixed + term
        real, imag = parts(near, f)
        line = jnp.sum(real * mixed[:, :tile] + imag * mixed[:, tile:], axis=0, keepdims=True)
        tot[pl.ds(f, 1), :] = line

    resid_lag, grad_lag = 1, 2

    def self_one(f, carry):
        stage_self(f)
        return carry

    lax.fori_loop(0, freqs, self_one, 0)
    for k in range(1, tiles):
        self_corr_copy(k).start()

    def step(s, carry):
        @pl.when(s < freqs)
        def _():
            stage_cross(s)

        @pl.when(s == resid_lag)
        def _():
            for d in range(1, reach + 1):
                pay_copy(d).wait_recv()
            self_resid()

        @pl.when(s == grad_lag)
        def _():
            for k in range(1, tiles):
                self_resid_copy(k, lax.rem(mine + tiles - k, tiles)).wait_recv()

        @pl.when(jnp.logical_and(s >= resid_lag, s < freqs + resid_lag))
        def _():
            stage_resid(s - resid_lag)

        @pl.when(s >= grad_lag)
        def _():
            stage_grad(s - grad_lag)

        return carry

    lax.fori_loop(0, freqs + grad_lag, step, 0)

    for k in range(1, stations):
        total_copy(k).start()
    keep_own = pltpu.make_async_copy(tot, out_ref.at[0], own_sem)
    keep_own.start()

    def drain(f, carry):
        for d in range(1, reach + 1):
            green_copy(d, f).wait_send()
        for k in range(1, tiles):
            corr_copy(k, f).wait_send()
            resid_copy(k, f, mine).wait_send()
        return carry

    lax.fori_loop(0, freqs, drain, 0)
    for d in range(1, reach + 1):
        pay_copy(d).wait_send()
    for k in range(1, tiles):
        self_corr_copy(k).wait_send()
        self_resid_copy(k, mine).wait_send()
    keep_own.wait()
    for k in range(1, stations):
        total_copy(k).wait_recv()
    for k in range(1, stations):
        total_copy(k).wait_send()


def shards(green_spectra, source_power, partners, observed, region):
    stations = lax.axis_size("sta")
    tiles = lax.axis_size("grid")
    reach = min(MAX_REACH, (stations - 1) // 2)
    freqs, block, _, tile = green_spectra.shape
    pairs = partners.shape[1]
    cols = tile // 128
    own_rows = block // tiles
    slots = reach + 1
    c_scale = 1.0 / math.sqrt(tile * tiles)
    out_scale = c_scale / math.sqrt(pairs * block)
    green = green_spectra.reshape(freqs, block, 2, cols, 128)
    green = green.transpose(0, 1, 3, 2, 4).reshape(freqs, block * cols * 2, 128)
    dma = pltpu.SemaphoreType.DMA
    totals = pl.pallas_call(
        functools.partial(kernel, stations, tiles, reach, c_scale),
        out_shape=jax.ShapeDtypeStruct((stations, freqs, tile), F32),
        in_specs=[pl.BlockSpec(memory_space=pl.ANY)] * 4,
        out_specs=pl.BlockSpec(memory_space=pl.ANY),
        scratch_shapes=[
            pltpu.VMEM(source_power.shape, F32),
            pltpu.SMEM(partners.shape, jnp.int32),
            pltpu.VMEM(observed.shape, F32),
            pltpu.VMEM(green.shape, F32),
            pltpu.VMEM((freqs, 2, block, 2 * tile), BF16),
            pltpu.VMEM((reach,) + green.shape, F32),
            pltpu.VMEM((slots, freqs, 2, 2 * block, 2 * tile), BF16),
            pltpu.VMEM((tiles, freqs, own_rows, 2 * block), F32),
            pltpu.VMEM((tiles, freqs, own_rows, 2 * block), F32),
            pltpu.VMEM((tiles, freqs, own_rows, 2 * block), F32),
            pltpu.VMEM((freqs, tiles, reach, own_rows, 2 * block), F32),
            pltpu.VMEM((freqs, tiles, reach, own_rows, 2 * block), F32),
            pltpu.VMEM((freqs, tiles, reach, own_rows, 2 * block), F32),
            pltpu.VMEM((2 * block, 2 * block), F32),
            pltpu.VMEM((reach, freqs + 1, own_rows, 2 * block), F32),
            pltpu.VMEM((reach, freqs + 1, own_rows, 2 * block), F32),
            pltpu.VMEM((freqs, tile), F32),
            dma,
            dma((3,)),
            dma,
            dma((reach, freqs)), dma((reach, freqs)),
            dma((reach,)), dma((reach,)),
            dma((tiles,)), dma((tiles,)),
            dma((tiles,)), dma((tiles,)),
            dma((tiles, freqs)), dma((tiles, freqs)),
            dma((tiles, freqs)), dma((tiles, freqs)),
            dma((stations,)), dma((stations,)),
        ],
        compiler_params=pltpu.CompilerParams(
            collective_id=0, has_side_effects=True, vmem_limit_bytes=60 * 1024 * 1024
        ),
    )(green, source_power, partners, observed)
    mask = jnp.repeat(region.astype(F32), MBLK)
    summed = totals[0]
    for k in range(1, stations):
        summed = summed + totals[k]
    return summed * (out_scale * mask)[None, :]


def solution(mesh):
    in_specs = (
        P("band", "sta", None, "grid"),
        P("band", "grid"),
        P("sta", None),
        P("sta", None, "band", None, None),
        P(("band", "grid")),
    )
    out_specs = P("band", "grid")
    return jax.shard_map(shards, mesh=mesh, in_specs=in_specs, out_specs=out_specs, check_vma=False)
```

```python
import functools
import math

import jax
import jax.numpy as jnp
from jax import lax
from jax.experimental import pallas as pl
from jax.experimental.pallas import tpu as pltpu
from jax.sharding import PartitionSpec as P

MBLK = 128
MAX_REACH = 4
MESH = pl.DeviceIdType.MESH
F32 = jnp.float32
BF16 = jnp.bfloat16


def split(x):
    high = x.astype(BF16)
    return high, (x - high.astype(F32)).astype(BF16)


def dot3(left, right, contract):
    dot = functools.partial(
        lax.dot_general, dimension_numbers=(contract, ((), ())), preferred_element_type=F32
    )
    return dot(left[0], right[0]) + dot(left[0], right[1]) + dot(left[1], right[0])


def kernel(
    stations, tiles, reach, c_scale,
    g_hbm, power_hbm, partners_hbm, obs_hbm, out_ref,
    power_ref, partners_ref, obs_ref, near, lefts, far, wide, cself, cselfrecv, rself, cpart, crecv, rfull, flip, pay, payrecv, tot,
    load_sem, small_sem, own_sem, g_send, g_recv, pay_send, pay_recv, cs_send, cs_recv, rs_send, rs_recv,
    c_send, c_recv, r_send, r_recv, t_send, t_recv,
):
    freqs, rows, _ = g_hbm.shape
    block = obs_ref.shape[3]
    pairs = obs_ref.shape[1]
    cols = rows // (2 * block)
    tile = cols * 128
    own_rows = block // tiles
    me = lax.axis_index("sta")
    mine = lax.axis_index("grid")
    first = pl.multiple_of(mine * own_rows, own_rows)

    barrier = pltpu.get_barrier_semaphore()
    for k in range(1, stations):
        pl.semaphore_signal(
            barrier, inc=1, device_id={"sta": lax.rem(me + k, stations)}, device_id_type=MESH
        )
    for k in range(1, tiles):
        pl.semaphore_signal(
            barrier, inc=1, device_id={"grid": lax.rem(mine + k, tiles)}, device_id_type=MESH
        )

    load = pltpu.make_async_copy(g_hbm, near, load_sem)
    load.start()
    small = [
        pltpu.make_async_copy(source, target, small_sem.at[number])
        for number, (source, target) in enumerate((
            (partners_hbm, partners_ref), (obs_hbm, obs_ref),
            (power_hbm, power_ref),
        ))
    ]
    for copy in small:
        copy.start()

    pl.semaphore_wait(barrier, stations - 1 + tiles - 1)

    def green_copy(d, f):
        return pltpu.make_async_remote_copy(
            src_ref=g_hbm.at[f], dst_ref=far.at[d - 1, f],
            send_sem=g_send.at[d - 1, f], recv_sem=g_recv.at[d - 1, f],
            device_id={"sta": lax.rem(me + d, stations)}, device_id_type=MESH,
        )

    def pay_copy(d):
        return pltpu.make_async_remote_copy(
            src_ref=pay.at[d - 1], dst_ref=payrecv.at[d - 1],
            send_sem=pay_send.at[d - 1], recv_sem=pay_recv.at[d - 1],
            device_id={"sta": lax.rem(me + d, stations)}, device_id_type=MESH,
        )

    def corr_copy(k, f):
        peer = lax.rem(mine + k, tiles)
        return pltpu.make_async_remote_copy(
            src_ref=cpart.at[f, peer], dst_ref=crecv.at[f, k],
            send_sem=c_send.at[k, f], recv_sem=c_recv.at[k, f],
            device_id={"grid": peer}, device_id_type=MESH,
        )

    def resid_copy(k, f, owner):
        return pltpu.make_async_remote_copy(
            src_ref=rfull.at[f, owner], dst_ref=rfull.at[f, owner],
            send_sem=r_send.at[k, f], recv_sem=r_recv.at[k, f],
            device_id={"grid": lax.rem(mine + k, tiles)}, device_id_type=MESH,
        )

    def self_corr_copy(k):
        peer = lax.rem(mine + k, tiles)
        return pltpu.make_async_remote_copy(
            src_ref=cself.at[peer], dst_ref=cselfrecv.at[k],
            send_sem=cs_send.at[k], recv_sem=cs_recv.at[k],
            device_id={"grid": peer}, device_id_type=MESH,
        )

    def self_resid_copy(k, owner):
        return pltpu.make_async_remote_copy(
            src_ref=rself.at[owner], dst_ref=rself.at[owner],
            send_sem=rs_send.at[k], recv_sem=rs_recv.at[k],
            device_id={"grid": lax.rem(mine + k, tiles)}, device_id_type=MESH,
        )

    def total_copy(k):
        return pltpu.make_async_remote_copy(
            src_ref=tot, dst_ref=out_ref.at[k],
            send_sem=t_send.at[k], recv_sem=t_recv.at[k],
            device_id={"sta": lax.rem(me + k, stations)}, device_id_type=MESH,
        )

    def listed(q, target):
        return jnp.where(partners_ref[0, q] == target, 1.0, 0.0).astype(F32)

    early = min(2, freqs)
    for f in range(early):
        for d in range(1, reach + 1):
            green_copy(d, f).start()

    for copy in small:
        copy.wait()

    lane = lax.broadcasted_iota(jnp.int32, (own_rows, 2 * block), 1)
    sign = jnp.where(lane < block, 1.0, -1.0).astype(F32)
    for d in range(1, reach + 1):
        target = lax.rem(me + d, stations)
        flags = [listed(q, target) for q in range(pairs)]

        def flip_one(f, carry):
            chosen = flags[0] * obs_ref[0, 0, f]
            for q in range(1, pairs):
                chosen = chosen + flags[q] * obs_ref[0, q, f]
            square = jnp.concatenate([chosen, pltpu.roll(chosen, block, 1)], axis=0)
            flip[...] = square.T
            pay[d - 1, f] = flip[pl.ds(first, own_rows), :] * sign
            return carry

        lax.fori_loop(0, freqs, flip_one, 0)
        count = flags[0]
        for q in range(1, pairs):
            count = count + flags[q]
        pay[d - 1, freqs] = jnp.zeros((own_rows, 2 * block), F32) + count
        pay_copy(d).start()

    for f in range(early, freqs):
        for d in range(1, reach + 1):
            green_copy(d, f).start()

    load.wait()

    def parts(ref, f):
        out = []
        for part in range(2):
            pieces = [
                ref[f, pl.ds(2 * c + part, block, stride=2 * cols), :] for c in range(cols)
            ]
            out.append(jnp.concatenate(pieces, axis=1))
        return out

    def widen(real, imag, slot, f):
        rh, rl = split(real)
        ih, il = split(imag)
        for number, (re, im) in enumerate(((rh, ih), (rl, il))):
            wide[slot, f, number, 0:block] = jnp.concatenate([re, im], axis=1)
            wide[slot, f, number, block : 2 * block] = jnp.concatenate([-im, re], axis=1)

    def correlate(left, slot, f):
        right = (wide[slot, f, 0], wide[slot, f, 1])
        whole = dot3(left, right, ((1,), (1,))) * c_scale
        for k in range(tiles):
            piece = whole[k * own_rows : (k + 1) * own_rows]
            if slot == 0:
                cself[k, f] = piece
            else:
                cpart[f, k, slot - 1] = piece

    def stage_self(f):
        real, imag = parts(near, f)
        power = power_ref[pl.ds(f, 1), :]
        widen(real, imag, 0, f)
        high, low = split(jnp.concatenate([real * power, imag * power], axis=1))
        lefts[f, 0] = high
        lefts[f, 1] = low
        correlate((high, low), 0, f)

    def stage_cross(f):
        left = (lefts[f, 0], lefts[f, 1])
        for d in range(1, reach + 1):
            green_copy(d, f).wait_recv()
            real, imag = parts(far.at[d - 1], f)
            widen(real, imag, d, f)
            correlate(left, d, f)
        for k in range(1, tiles):
            corr_copy(k, f).start()

    row = lax.broadcasted_iota(jnp.int32, (own_rows, 2 * block), 0) + mine * own_rows
    keep = jnp.where(lax.rem(lane, block) == row, 0.0, 1.0).astype(F32)

    def observed_rows(f, target):
        chosen = listed(0, target) * obs_ref[0, 0, f, pl.ds(first, own_rows), :]
        for q in range(1, pairs):
            chosen = chosen + listed(q, target) * obs_ref[0, q, f, pl.ds(first, own_rows), :]
        return chosen

    def self_resid():
        for k in range(1, tiles):
            self_corr_copy(k).wait_recv()

        def one(f, carry):
            total = cself[mine, f]
            for k in range(1, tiles):
                total = total + cselfrecv[k, f]
            rself[mine, f] = (total - observed_rows(f, me)) * keep
            return carry

        lax.fori_loop(0, freqs, one, 0)
        for k in range(1, tiles):
            self_resid_copy(k, mine).start()

    def stage_resid(f):
        for k in range(1, tiles):
            corr_copy(k, f).wait_recv()
        for d in range(1, reach + 1):
            total = cpart[f, mine, d - 1]
            for k in range(1, tiles):
                total = total + crecv[f, k, d - 1]
            target = lax.rem(me + stations - d, stations)
            weight = payrecv[d - 1, freqs]
            for q in range(pairs):
                weight = weight + listed(q, target)
            seen = observed_rows(f, target) + payrecv[d - 1, f]
            rfull[f, mine, d - 1] = weight * total - seen
        for k in range(1, tiles):
            resid_copy(k, f, mine).start()

    def stage_grad(f):
        for k in range(1, tiles):
            resid_copy(k, f, lax.rem(mine + tiles - k, tiles)).wait_recv()
        mixed = None
        for slot in range(reach + 1):
            pieces = [rself[k, f] if slot == 0 else rfull[f, k, slot - 1] for k in range(tiles)]
            resid = jnp.concatenate(pieces, axis=0)
            term = dot3(split(resid), (wide[slot, f, 0], wide[slot, f, 1]), ((1,), (0,)))
            mixed = term if mixed is None else mixed + term
        real, imag = parts(near, f)
        line = jnp.sum(real * mixed[:, :tile] + imag * mixed[:, tile:], axis=0, keepdims=True)
        tot[pl.ds(f, 1), :] = line

    resid_lag, grad_lag = 1, 2

    def self_one(f, carry):
        stage_self(f)
        return carry

    lax.fori_loop(0, freqs, self_one, 0)
    for k in range(1, tiles):
        self_corr_copy(k).start()

    def step(s, carry):
        @pl.when(s < freqs)
        def _():
            stage_cross(s)

        @pl.when(s == resid_lag)
        def _():
            for d in range(1, reach + 1):
                pay_copy(d).wait_recv()
            self_resid()

        @pl.when(s == grad_lag)
        def _():
            for k in range(1, tiles):
                self_resid_copy(k, lax.rem(mine + tiles - k, tiles)).wait_recv()

        @pl.when(jnp.logical_and(s >= resid_lag, s < freqs + resid_lag))
        def _():
            stage_resid(s - resid_lag)

        @pl.when(s >= grad_lag)
        def _():
            stage_grad(s - grad_lag)

        return carry

    lax.fori_loop(0, freqs + grad_lag, step, 0)

    for k in range(1, stations):
        total_copy(k).start()
    keep_own = pltpu.make_async_copy(tot, out_ref.at[0], own_sem)
    keep_own.start()

    def drain(f, carry):
        for d in range(1, reach + 1):
            green_copy(d, f).wait_send()
        for k in range(1, tiles):
            corr_copy(k, f).wait_send()
            resid_copy(k, f, mine).wait_send()
        return carry

    lax.fori_loop(0, freqs, drain, 0)
    for d in range(1, reach + 1):
        pay_copy(d).wait_send()
    for k in range(1, tiles):
        self_corr_copy(k).wait_send()
        self_resid_copy(k, mine).wait_send()
    keep_own.wait()
    for k in range(1, stations):
        total_copy(k).wait_recv()
    for k in range(1, stations):
        total_copy(k).wait_send()


def shards(green_spectra, source_power, partners, observed, region):
    stations = lax.axis_size("sta")
    tiles = lax.axis_size("grid")
    reach = min(MAX_REACH, (stations - 1) // 2)
    freqs, block, _, tile = green_spectra.shape
    pairs = partners.shape[1]
    cols = tile // 128
    own_rows = block // tiles
    slots = reach + 1
    c_scale = 1.0 / math.sqrt(tile * tiles)
    out_scale = c_scale / math.sqrt(pairs * block)
    green = green_spectra.reshape(freqs, block, 2, cols, 128)
    green = green.transpose(0, 1, 3, 2, 4).reshape(freqs, block * cols * 2, 128)
    dma = pltpu.SemaphoreType.DMA
    totals = pl.pallas_call(
        functools.partial(kernel, stations, tiles, reach, c_scale),
        out_shape=jax.ShapeDtypeStruct((stations, freqs, tile), F32),
        in_specs=[pl.BlockSpec(memory_space=pl.ANY)] * 4,
        out_specs=pl.BlockSpec(memory_space=pl.ANY),
        scratch_shapes=[
            pltpu.VMEM(source_power.shape, F32),
            pltpu.SMEM(partners.shape, jnp.int32),
            pltpu.VMEM(observed.shape, F32),
            pltpu.VMEM(green.shape, F32),
            pltpu.VMEM((freqs, 2, block, 2 * tile), BF16),
            pltpu.VMEM((reach,) + green.shape, F32),
            pltpu.VMEM((slots, freqs, 2, 2 * block, 2 * tile), BF16),
            pltpu.VMEM((tiles, freqs, own_rows, 2 * block), F32),
            pltpu.VMEM((tiles, freqs, own_rows, 2 * block), F32),
            pltpu.VMEM((tiles, freqs, own_rows, 2 * block), F32),
            pltpu.VMEM((freqs, tiles, reach, own_rows, 2 * block), F32),
            pltpu.VMEM((freqs, tiles, reach, own_rows, 2 * block), F32),
            pltpu.VMEM((freqs, tiles, reach, own_rows, 2 * block), F32),
            pltpu.VMEM((2 * block, 2 * block), F32),
            pltpu.VMEM((reach, freqs + 1, own_rows, 2 * block), F32),
            pltpu.VMEM((reach, freqs + 1, own_rows, 2 * block), F32),
            pltpu.VMEM((freqs, tile), F32),
            dma,
            dma((3,)),
            dma,
            dma((reach, freqs)), dma((reach, freqs)),
            dma((reach,)), dma((reach,)),
            dma((tiles,)), dma((tiles,)),
            dma((tiles,)), dma((tiles,)),
            dma((tiles, freqs)), dma((tiles, freqs)),
            dma((tiles, freqs)), dma((tiles, freqs)),
            dma((stations,)), dma((stations,)),
        ],
        compiler_params=pltpu.CompilerParams(
            collective_id=0, has_side_effects=True, vmem_limit_bytes=60 * 1024 * 1024
        ),
    )(green, source_power, partners, observed)
    mask = jnp.repeat(region.astype(F32), MBLK)
    return jnp.sum(totals, axis=0) * out_scale * mask[None, :]


def solution(mesh):
    in_specs = (
        P("band", "sta", None, "grid"),
        P("band", "grid"),
        P("sta", None),
        P("sta", None, "band", None, None),
        P(("band", "grid")),
    )
    out_specs = P("band", "grid")
    return jax.shard_map(shards, mesh=mesh, in_specs=in_specs, out_specs=out_specs, check_vma=False)
```
